128 devices in a mesh: section: 2 (over core), dp: 16 (over y, x), expert: 4 (over z).
Axes of the slice: x: 4, y: 4, z: 4, core: 2. Of those that a mesh axis runs over, the one named last changes fastest.
Arguments:
- inputs: bfloat16 [2, 1024, 3072], P(None, 'dp'), may hold values from -6 to 6
- cotangent: bfloat16 [2, 1024, 3072], P(None, 'dp'), may hold values from -1.5 to 1.5
- gain: bfloat16 [2, 3072], P('section'), may hold values from 0.099609375 to 1.8984375
- w_up: bfloat16 [2, 16, 5376, 3072], P('section', 'dp', 'expert'), may hold values from -0.109375 to 0.109375
- w_down: bfloat16 [2, 16, 5376, 3072], P('section', 'dp', 'expert'), may hold values from -0.078125 to 0.078125
- expert_ids: int32 [2, 2, 1024, 6], P('section', None, 'dp'), may hold values from 0 to 15, all different within a row; in each aligned block of 64 rows (0 to 63, 64 to 127, ..., all dimensions but the last counted through in order) at most 25 rows name the same one
- expert_counts: int32 [2, 2, 1024], P('section', None, 'dp'), may hold values from 5 to 6
- combine_fixed: int32 [2, 2, 1024, 6], P('section', None, 'dp'), may hold values from 1024 to 4096
Outputs:
- outputs: bfloat16 [2, 2, 1024, 3072], P('section', None, 'dp')
- input_grads: bfloat16 [2, 2, 1024, 3072], P('section', None, 'dp')
- grad_gain: float32 [2, 3072], P('section', 'dp')
The draws below stay inside these ranges and needn't reach their ends.
Inputs may be any that keep to these rules, and one draw needn't show every extreme that they name: `expert_ids`: each token's 6 slots name different experts. In the 64 tokens of one index of dp in one microbatch (aligned blocks of 64 rows), no expert is named by more than 25 slots, used or not, and in some blocks one expert is named by exactly 25. Only the first expert_counts slots of a token are used.
All inputs are finite; a program needn't handle non-finite values.
Results may differ from the reference program's by a relative error of at most 0.013.
Values may be sent and summed in bfloat16 or wider, within the bound.
No kernel may reach another device: no remote copies, remote signals or barrier semaphores. Data moves between devices by JAX's collectives and lax.ppermute only.
A program may use at most 128 MiB of HBM per device.

```python
import math
from functools import partial
import jax
import jax.numpy as jnp
import numpy as np
from jax import lax

D = 3072
FF = 5376
MICRO = 2
ROWS = 64
LAYERS = 2
EXPERTS = 16
TOP = 6
CAP = 25
TOKENS = 1024
N_DP = 16
N_EXPERT = 4


def set_ends(result, key, low, high):
    longest = result.shape.index(max(result.shape))
    spots = []
    for shift in (0, 1):
        where = [jax.random.randint(jax.random.fold_in(key, axis), (), 0, length) for axis, length in enumerate(result.shape)]
        where[longest] = (where[longest] + shift) % result.shape[longest]
        spots.append(tuple(where))
    return result.at[spots[0]].set(low).at[spots[1]].set(high)


def levels(rng, dims, shards, smallest, high):
    def one(axis_at, blocks):
        steps = jax.random.uniform(jax.random.fold_in(jax.random.fold_in(rng, 6), axis_at), (blocks,), jnp.float32, smallest / len(shards), high / len(shards))
        return jnp.repeat(jnp.exp(steps), dims[axis_at] // blocks).reshape((-1,) + (1,) * (len(dims) - axis_at - 1))

    level = one(*shards[0])
    for cut in shards[1:]:
        level = level * one(*cut)
    return level


def routed_block(stream_key, own, number, rows, amount, top, bound, skew):
    ranking = jax.random.permutation(stream_key, amount)
    heavy_load, common = portions_of(amount, rows * top, bound, skew, True), portions_of(amount, rows * top, bound, skew, False)
    places = jnp.arange(amount)

    def named(tallies, rotation):
        used = int((tallies > 0).sum())
        fixed = max(1, used // 4)
        shifted = fixed + (places - fixed + rotation * (used - fixed)) % max(1, amount - fixed)
        return jnp.zeros((amount,), jnp.int32).at[ranking[jnp.where(places < fixed, places, shifted)]].set(jnp.asarray(tallies, jnp.int32))

    tallies = jnp.where(number % 4 == 0, named(heavy_load, number // 4), named(common, number - number // 4 - 1))
    mixed = jax.random.permutation(jax.random.fold_in(own, 3), amount)
    donor, taker = mixed[0:amount // 2 * 2:2], mixed[1:amount // 2 * 2:2]
    margin = jnp.minimum(tallies[donor] - 1, bound - tallies[taker]) // 2
    margin = jnp.where((donor == ranking[0]) | (taker == ranking[0]) | (tallies[taker] == 0), 0, jnp.maximum(margin, 0))
    shifted = jax.random.randint(jax.random.fold_in(own, 4), (amount // 2,), 0, 1 << 20) % (margin + 1)
    tallies = tallies.at[donor].add(-shifted).at[taker].add(shifted)
    items = jnp.searchsorted(jnp.cumsum(tallies), jnp.arange(rows * top), side="right").astype(jnp.int32)
    table = items.reshape(top, rows).T
    table = table[jax.random.permutation(jax.random.fold_in(own, 1), rows)]
    rotation = jax.random.randint(jax.random.fold_in(own, 2), (rows, 1), 0, top)
    return jnp.take_along_axis(table, (jnp.arange(top)[None, :] + rotation) % top, axis=1)


def portions_of(count, total, bound, lean, full):
    loads = [(1 << 20) // math.isqrt(standing ** lean) + 1 for standing in range(1, count + 1)]
    largest = bound if full else min(bound, max(-(-total // count), total * loads[0] // sum(loads)))
    least = 1 if total - largest >= count - 1 else 0
    given, rest = [largest] + [least] * (count - 1), total - largest - least * (count - 1)
    while rest > 0:
        candidates = [i for i in range(1, count) if given[i] < largest] or [i for i in range(1, count) if given[i] < bound]
        mass, left = sum([loads[i] for i in candidates]), rest
        for i in candidates:
            more = min(bound - given[i], max(1, left * loads[i] // mass), rest)
            given[i] = given[i] + more
            rest = rest - more
    return np.array(given)


def scatter_about(rng, shape, scale, limit, cuts=(), held_as=jnp.bfloat16):
    values = scale * jax.random.normal(rng, shape, jnp.float32)
    if cuts:
        values = values * levels(rng, shape, cuts, -0.22, 0.18)
    return jnp.clip(values, -limit, limit).astype(held_as)


def setup_inputs(seed: int = 0) -> dict:
    splits = jax.random.split(jax.random.key(seed), 9)
    inputs = scatter_about(splits[0], (MICRO, TOKENS, D), 1.0, 6.0, ((1, 16),))
    cotangent = scatter_about(splits[1], (MICRO, TOKENS, D), 0.25, 1.5, ((1, 16),))
    gain = jnp.clip(1.0 + 0.18 * jax.random.normal(splits[2], (LAYERS, D), jnp.float32), 0.099609375, 1.8984375).astype(jnp.bfloat16)
    w_up = scatter_about(splits[3], (LAYERS, EXPERTS, FF, D), D ** -0.5, 0.109375, ((0, 2), (1, 16), (2, 4)))
    w_down = scatter_about(splits[4], (LAYERS, EXPERTS, FF, D), FF ** -0.5, 0.078125, ((0, 2), (1, 16), (2, 4)))
    expert_ids_keys = jax.random.split(jax.random.fold_in(splits[5], 1), LAYERS * MICRO * TOKENS // ROWS)
    expert_ids_turns = jax.random.permutation(jax.random.fold_in(splits[5], 3), LAYERS * MICRO * TOKENS // ROWS)
    expert_ids = jax.vmap(lambda own, number: routed_block(jax.random.fold_in(splits[5], 2), own, number, ROWS, EXPERTS, TOP, CAP, 2))(expert_ids_keys, expert_ids_turns).reshape((LAYERS, MICRO, TOKENS, TOP))
    expert_counts = set_ends(jax.random.randint(splits[6], (LAYERS, MICRO, TOKENS), max(1, TOP - 1), TOP + 1), jax.random.fold_in(splits[6], 1), max(1, TOP - 1), TOP).astype(jnp.int32)
    combine_fixed = set_ends(jax.random.randint(splits[7], (LAYERS, MICRO, TOKENS, TOP), 1024, 4097), jax.random.fold_in(splits[7], 1), 1024, 4096).astype(jnp.int32)
    return {"inputs": inputs, "cotangent": cotangent, "gain": gain, "w_up": w_up, "w_down": w_down, "expert_ids": expert_ids, "expert_counts": expert_counts, "combine_fixed": combine_fixed}


EPSILON = 1e-05
PRECISE = lax.Precision.HIGHEST

def slot_tables(expert_index, counts, fixed, experts, capacity):
    row_count, top_count = expert_index.shape
    is_live = jnp.arange(top_count)[None, :] < counts[:, None]
    shares = jnp.where(is_live, fixed.astype(jnp.float32), 0.0)
    weights = shares / lax.optimization_barrier(jnp.sum(shares, axis=1, keepdims=True))
    flattened = expert_index.reshape(-1)
    onehot = (flattened[:, None] == jnp.arange(experts)[None, :]).astype(jnp.int32)
    before = jnp.cumsum(onehot, axis=0) - onehot
    position = lax.optimization_barrier(jnp.sum(before * onehot, axis=1))
    target = flattened * capacity + position
    placing = (target[:, None] == jnp.arange(experts * capacity)[None, :]).astype(jnp.float32)
    owners = jnp.arange(row_count * top_count) // top_count
    token_hot = (owners[:, None] == jnp.arange(row_count)[None, :]).astype(jnp.float32)
    selector = jnp.dot(placing.T, token_hot, precision=PRECISE)
    slot_weights = jnp.dot(placing.T, weights.reshape(-1), precision=PRECISE)
    return (selector, slot_weights)

def group_sum(parts):
    kept = lax.optimization_barrier(parts)
    return lax.optimization_barrier(jnp.sum(kept.astype(jnp.float32), axis=0))

def expert_forward(expert_item):
    arrived_rows, up_rows, down_rows = expert_item
    pre_act = jnp.einsum('msc,fc->msf', arrived_rows.astype(jnp.float32), up_rows.astype(jnp.float32), precision=PRECISE)
    activated = jax.nn.silu(pre_act).astype(jnp.bfloat16)
    grouped = activated.reshape(activated.shape[0], activated.shape[1], N_EXPERT, FF // N_EXPERT)
    down_grouped = down_rows.reshape(N_EXPERT, FF // N_EXPERT, D)
    parts = jnp.einsum('msjf,jfc->jmsc', grouped.astype(jnp.float32), down_grouped.astype(jnp.float32), precision=PRECISE).astype(jnp.bfloat16)
    return (pre_act, group_sum(parts))

def expert_backward(expert_item):
    d_out, pre_act, up_rows, down_rows = expert_item
    d_act = jnp.einsum('msc,fc->msf', d_out.astype(jnp.float32), down_rows.astype(jnp.float32), precision=PRECISE)
    logistic = jax.nn.sigmoid(pre_act)
    d_pre = (d_act * logistic * (1.0 + pre_act * (1.0 - logistic))).astype(jnp.bfloat16)
    grouped = d_pre.reshape(d_pre.shape[0], d_pre.shape[1], N_EXPERT, FF // N_EXPERT)
    up_grouped = up_rows.reshape(N_EXPERT, FF // N_EXPERT, D)
    parts = jnp.einsum('msjf,jfc->jmsc', grouped.astype(jnp.float32), up_grouped.astype(jnp.float32), precision=PRECISE).astype(jnp.bfloat16)
    return group_sum(parts)

def reference(inputs, cotangent, gain, w_up, w_down, expert_ids, expert_counts, combine_fixed):
    split_shape = (MICRO, N_DP, ROWS)

    def to_blocks(array):
        return array.reshape(split_shape + array.shape[2:])

    def to_expert(home):
        width_last = home.shape[-1]
        split_view = home.reshape(MICRO, N_DP, EXPERTS, CAP, width_last)
        return jnp.transpose(split_view, (2, 0, 1, 3, 4)).reshape(EXPERTS, MICRO, N_DP * CAP, width_last)

    def to_home(side):
        width_last = side.shape[-1]
        split_view = side.reshape(EXPERTS, MICRO, N_DP, CAP, width_last)
        return jnp.transpose(split_view, (1, 2, 0, 3, 4)).reshape(MICRO, N_DP, EXPERTS * CAP, width_last)
    table_fn = jax.vmap(jax.vmap(partial(slot_tables, experts=EXPERTS, capacity=CAP)))
    current = to_blocks(inputs)
    saved = []
    layer_outputs = []
    for layer_index in range(LAYERS):
        selector, slot_weight = table_fn(to_blocks(expert_ids[layer_index]), to_blocks(expert_counts[layer_index]), to_blocks(combine_fixed[layer_index]))
        gain_row = gain[layer_index].astype(jnp.float32)
        state_f = current.astype(jnp.float32)
        inverse_rms = lax.rsqrt(lax.optimization_barrier(jnp.mean(state_f * state_f, axis=-1, keepdims=True)) + EPSILON)
        normed = (state_f * inverse_rms * gain_row).astype(jnp.bfloat16)
        outgoing = jnp.einsum('mpsr,mprc->mpsc', selector, normed.astype(jnp.float32), precision=PRECISE).astype(jnp.bfloat16)
        arrived = to_expert(outgoing)
        pre_act, summed = lax.map(expert_forward, (arrived, w_up[layer_index], w_down[layer_index]))
        returned = to_home(summed) * slot_weight[..., None]
        mixture = jnp.einsum('mpsr,mpsc->mprc', selector, returned, precision=PRECISE)
        following = (state_f + mixture).astype(jnp.bfloat16)
        saved.append((current, selector, slot_weight, pre_act))
        layer_outputs.append(following.reshape(MICRO, TOKENS, D))
        current = following
    upstream = to_blocks(cotangent)
    input_list = [None] * LAYERS
    gain_list = [None] * LAYERS
    for layer_index in reversed(range(LAYERS)):
        current, selector, slot_weight, pre_act = saved[layer_index]
        gain_row = gain[layer_index].astype(jnp.float32)
        spread = jnp.einsum('mpsr,mprc->mpsc', selector, upstream.astype(jnp.float32), precision=PRECISE) * slot_weight[..., None]
        d_out = to_expert(spread.astype(jnp.bfloat16))
        d_summed = lax.map(expert_backward, (d_out, pre_act, w_up[layer_index], w_down[layer_index]))
        d_norm = jnp.einsum('mpsr,mpsc->mprc', selector, to_home(d_summed), precision=PRECISE)
        state_f = current.astype(jnp.float32)
        inverse_rms = lax.rsqrt(lax.optimization_barrier(jnp.mean(state_f * state_f, axis=-1, keepdims=True)) + EPSILON)
        scaled = state_f * inverse_rms
        d_scaled = d_norm * gain_row
        d_input = inverse_rms * (d_scaled - scaled * lax.optimization_barrier(jnp.mean(d_scaled * scaled, axis=-1, keepdims=True)))
        preceding = (upstream.astype(jnp.float32) + d_input).astype(jnp.bfloat16)
        gain_list[layer_index] = lax.optimization_barrier(jnp.sum(d_norm * scaled, axis=(0, 1, 2)))
        input_list[layer_index] = preceding.reshape(MICRO, TOKENS, D)
        upstream = preceding
    return (jnp.stack(layer_outputs), jnp.stack(input_list), jnp.stack(gain_list))
```

```python
import jax
import jax.numpy as jnp
import numpy as np
from jax import lax
from jax.sharding import PartitionSpec as P

EPSILON = 1e-05
SWAP = [(0, 1), (1, 0)]
LANES = 128


def swapped(x):
    return lax.ppermute(x, "section", SWAP)


def normalize(current):
    state_f = current.astype(jnp.float32)
    inverse_rms = lax.rsqrt(jnp.mean(state_f * state_f, axis=-1, keepdims=True) + EPSILON)
    return state_f, inverse_rms


def shards(inputs, cotangent, gain, w_up, w_down, expert_ids, expert_counts, combine_fixed):
    section = lax.axis_index("section")
    owners = lax.axis_size("dp")
    ring = lax.axis_size("expert")
    row_count, width = inputs.shape[1:]
    top = expert_ids.shape[3]
    capacity = min(row_count, row_count * top // owners + 1)
    whole = capacity - 1
    main_rows = owners * whole
    bf16, f32 = jnp.bfloat16, jnp.float32

    up_own, down_own = w_up[0, 0], w_down[0, 0]
    first = section == 0

    def pick(mine, other, layer):
        return jnp.where(section == layer, mine, other)

    ints = jnp.concatenate([expert_ids[0], expert_counts[0][..., None], combine_fixed[0]], axis=-1)
    mine = lax.dynamic_index_in_dim(ints, section, 0, keepdims=False)
    theirs = swapped(lax.dynamic_index_in_dim(ints, 1 - section, 0, keepdims=False))
    gain_other = swapped(gain[0])
    gains = [pick(gain[0], gain_other, layer).astype(f32) for layer in range(2)]
    x0 = lax.dynamic_index_in_dim(inputs, section, 0, keepdims=False)
    upstream = lax.dynamic_index_in_dim(cotangent, section, 0, keepdims=False)
    up_other, down_other = swapped(up_own), swapped(down_own)

    column_owner = np.concatenate([np.repeat(np.arange(owners), whole), np.arange(owners)])
    column_place = np.concatenate([np.tile(np.arange(whole), owners), np.full(owners, whole)])
    spread = jnp.asarray(column_owner[None, :] == np.arange(owners)[:, None], bf16)
    place = jnp.asarray(column_place, f32)[None, :]
    below = jnp.asarray(np.tril(np.ones((row_count, row_count)), -1), bf16)

    def tables(packed):
        ids, counts, fixed = packed[:, :top], packed[:, top], packed[:, top + 1 :]
        live = jnp.arange(top)[None, :] < counts[:, None]
        shares = jnp.where(live, fixed.astype(f32), 0.0)
        shares = shares / jnp.sum(shares, axis=1, keepdims=True)
        named = ids[:, :, None] == jnp.arange(owners)[None, None, :]
        hot = jnp.sum(named.astype(f32), axis=1)
        share = jnp.sum(named.astype(f32) * shares[:, :, None], axis=1)
        before = jnp.dot(below, hot.astype(bf16), preferred_element_type=f32)
        hot_c = jnp.dot(hot.astype(bf16), spread, preferred_element_type=f32)
        before_c = jnp.dot(before.astype(bf16), spread, preferred_element_type=f32)
        share_c = jnp.dot(share.astype(bf16), spread, preferred_element_type=f32)
        chosen = hot_c * (before_c == place).astype(f32)
        return chosen.astype(bf16), (chosen * share_c).astype(bf16)

    plain, weighted = zip(*[tables(pick(mine, theirs, layer)) for layer in range(2)])

    def blocks(rows):
        head = rows[:main_rows].reshape(owners, whole, width)
        tail = rows[main_rows:].reshape(owners, whole, LANES)
        return jnp.concatenate([head, tail], axis=2)

    def unblocks(held):
        head = held[:, :, :width].reshape(main_rows, width)
        tail = held[:, :, width:].reshape(owners, width)
        return jnp.concatenate([head, tail], axis=0)

    def exchange(*rows):
        sent = [blocks(r) for r in rows]
        held = sent[0] if len(sent) == 1 else jnp.concatenate(sent, axis=1)
        back = lax.all_to_all(held, "dp", split_axis=0, concat_axis=0, tiled=True)
        return [unblocks(back[:, i * whole : (i + 1) * whole]) for i in range(len(rows))]

    def gathered(table, rows):
        return lax.dot_general(
            table, rows, (((0,), (0,)), ((), ())), preferred_element_type=f32
        ).astype(bf16)

    def over_groups(part):
        part = part.astype(bf16)
        near = [
            lax.ppermute(part, "expert", [(i, (i + by) % ring) for i in range(ring)])
            for by in (2, 1, 3)
        ]
        part, far, left, right = (v.astype(f32) for v in (part, *near))
        return (part + far) + (left + right)

    def home(table, rows):
        return over_groups(jnp.dot(table, rows, preferred_element_type=f32))

    def with_weights(layer, fn, *args):
        return lax.cond(
            section == layer,
            lambda uo, do, ux, dx, *a: fn(uo, do, *a),
            lambda uo, do, ux, dx, *a: fn(ux, dx, *a),
            up_own,
            down_own,
            up_other,
            down_other,
            *args,
        )

    def forward(up, down, rows):
        pre = lax.dot_general(rows, up, (((1,), (1,)), ((), ())), preferred_element_type=f32)
        activated = jax.nn.silu(pre).astype(bf16)
        return pre, jnp.dot(activated, down, preferred_element_type=f32).astype(bf16)

    def backward(up, down, rows, pre):
        d_act = lax.dot_general(rows, down, (((1,), (1,)), ((), ())), preferred_element_type=f32)
        logistic = jax.nn.sigmoid(pre)
        d_pre = (d_act * logistic * (1.0 + pre * (1.0 - logistic))).astype(bf16)
        return jnp.dot(d_pre, up, preferred_element_type=f32).astype(bf16)

    def forward_backward(up, down, rows, d_rows):
        pre, part = forward(up, down, rows)
        return part, backward(up, down, d_rows, pre)

    def normed_rows(current, layer):
        state_f, inverse_rms = normalize(current)
        return (state_f * inverse_rms * gains[layer]).astype(bf16)

    def finish(current, upstream, d_norm, layer):
        state_f, inverse_rms = normalize(current)
        scaled = state_f * inverse_rms
        d_scaled = d_norm * gains[layer]
        d_input = inverse_rms * (
            d_scaled - scaled * jnp.mean(d_scaled * scaled, axis=-1, keepdims=True)
        )
        return (upstream.astype(f32) + d_input).astype(bf16), jnp.sum(d_norm * scaled, axis=0)

    rows0, d_rows1 = exchange(
        gathered(plain[0], normed_rows(x0, 0)), gathered(weighted[1], upstream)
    )
    pre0, part0 = with_weights(0, forward, rows0)
    (back0,) = exchange(part0)
    x1 = (x0.astype(f32) + home(weighted[0], back0)).astype(bf16)
    (rows1,) = exchange(gathered(plain[1], normed_rows(x1, 1)))
    part1, d_part1 = with_weights(1, forward_backward, rows1, d_rows1)
    d_back1, back1 = exchange(d_part1, part1)
    grad1, gain1 = finish(x1, upstream, home(plain[1], d_back1), 1)
    (d_rows0,) = exchange(gathered(weighted[0], grad1))
    d_part0 = with_weights(0, backward, d_rows0, pre0)
    x2 = (x1.astype(f32) + home(weighted[1], back1)).astype(bf16)
    (d_back0,) = exchange(d_part0)
    grad0, gain0 = finish(x0, grad1, home(plain[0], d_back0), 0)

    kept = jnp.stack([pick(x1, x2, 0), pick(grad0, grad1, 0)])
    given = jnp.stack([pick(x2, x1, 0), pick(grad1, grad0, 0)])
    taken = swapped(given)
    low = jnp.where(first, kept, taken)
    high = jnp.where(first, taken, kept)
    both = jnp.stack([low, high], axis=1)
    gain_kept = pick(gain0, gain1, 0)
    gain_sum = gain_kept + swapped(pick(gain1, gain0, 0))
    slices = lax.all_to_all(
        gain_sum.reshape(owners, width // owners), "dp", split_axis=0, concat_axis=0, tiled=True
    )
    return both[0][None], both[1][None], jnp.sum(slices, axis=0)[None]


def solution(mesh):
    return jax.shard_map(
        shards,
        mesh=mesh,
        in_specs=(
            P(None, "dp", None),
            P(None, "dp", None),
            P("section", None),
            P("section", "dp", "expert", None),
            P("section", "dp", "expert", None),
            P("section", None, "dp", None),
            P("section", None, "dp"),
            P("section", None, "dp", None),
        ),
        out_specs=(
            P("section", None, "dp", None),
            P("section", None, "dp", None),
            P("section", "dp"),
        ),
        check_vma=False,
    )
```

```python
import functools

import jax
import jax.numpy as jnp
from jax import lax
from jax.experimental import pallas as pl
from jax.experimental.pallas import tpu as pltpu
from jax.sharding import PartitionSpec as P

EPSILON = 1e-05
SWAP = [(0, 1), (1, 0)]
LANES = 128
HIDDEN_STEP = 512
WIDTH_STEP = 512
VMEM_BYTES = 48 * 1024 * 1024
bf16, f32 = jnp.bfloat16, jnp.float32


def load_rows(held, rows, tails):
    owners, whole, wide = held.shape
    width = wide - LANES
    main = owners * whole
    rows[0:main, :] = held[:, :, 0:width].reshape(main, width)
    tails[...] = held[:, :, width:wide].astype(f32)
    for c in range(width // LANES):
        rows[main : main + owners, c * LANES : (c + 1) * LANES] = tails[:, c, :].astype(bf16)


def store_columns(out, tails, start, value):
    owners, whole, wide = out.shape
    main = owners * whole
    size = value.shape[1]
    out[:, :, start : start + size] = value[:main].astype(bf16).reshape(owners, whole, size)
    for c in range(size // LANES):
        tails[:, start // LANES + c, :] = value[main:, c * LANES : (c + 1) * LANES]


def store_tails(out, tails):
    wide = out.shape[2]
    out[:, :, wide - LANES : wide] = tails[...].astype(bf16)


def by_units(rows, weights):
    return lax.dot_general(rows, weights, (((1,), (1,)), ((), ())), preferred_element_type=f32)


def sigmoid(v):
    return 1.0 / (1.0 + jnp.exp(-v))


def chunks(size, step):
    return [(s, min(step, size - s)) for s in range(0, size, step)]


def expert_kernel(mode, layer, *refs):
    n_in = {"forward": 1, "backward": 3, "both": 2}[mode]
    n_out = 2
    helds, refs = refs[:n_in], refs[n_in:]
    own_hbm, other_hbm, refs = refs[:2], refs[2:4], refs[4:]
    outs, refs = refs[:n_out], refs[n_out:]
    up, down, rows, pre, act, tails, up_sem, down_sem = refs
    hidden, width = up.shape
    units = chunks(hidden, HIDDEN_STEP)
    columns = chunks(width, WIDTH_STEP)
    first, second = (down, up) if mode == "backward" else (up, down)

    def copies(src, dst, sem):
        return [
            pltpu.make_async_copy(src.at[pl.ds(s, n), :], dst.at[pl.ds(s, n), :], sem.at[i])
            for i, (s, n) in enumerate(units)
        ]

    def planned(pair):
        up_copies = copies(pair[0], up, up_sem)
        down_copies = copies(pair[1], down, down_sem)
        return (down_copies + up_copies) if mode == "backward" else (up_copies + down_copies)

    mine = lax.axis_index("section") == layer
    order = planned(own_hbm)

    @pl.when(mine)
    def _():
        for copy in order:
            copy.start()

    @pl.when(jnp.logical_not(mine))
    def _():
        for copy in planned(other_hbm):
            copy.start()

    early, late = order[: len(units)], order[len(units) :]

    load_rows(helds[0], rows, tails)
    for (s, n), copy in zip(units, early):
        copy.wait()
        v = by_units(rows[...], first[s : s + n, :])
        if mode == "backward":
            p = helds[1][:, s : s + n].astype(f32)
            g = sigmoid(p)
            act[:, s : s + n] = (v * g * (1.0 + p * (1.0 - g))).astype(bf16)
        else:
            pre[:, s : s + n] = v
            act[:, s : s + n] = (v * sigmoid(v)).astype(bf16)
    for copy in late:
        copy.wait()
    if mode == "backward":
        load_rows(helds[2], rows, tails)
    for s, n in columns:
        value = jnp.dot(act[...], second[:, s : s + n], preferred_element_type=f32)
        store_columns(outs[0], tails, s, value)
        if mode == "backward":
            terms = value * rows[:, s : s + n].astype(f32)
            outs[1][:, s : s + n] = jnp.sum(terms, axis=0, keepdims=True)
    store_tails(outs[0], tails)
    if mode == "forward":
        outs[1][...] = pre[...]
    if mode == "both":
        load_rows(helds[1], rows, tails)
        for s, n in units:
            v = by_units(rows[...], down[s : s + n, :])
            p = pre[:, s : s + n]
            g = sigmoid(p)
            act[:, s : s + n] = (v * g * (1.0 + p * (1.0 - g))).astype(bf16)
        for s, n in columns:
            store_columns(
                outs[1], tails, s, jnp.dot(act[...], up[:, s : s + n], preferred_element_type=f32)
            )
        store_tails(outs[1], tails)


def expert(mode, layer, weights, *inputs):
    hidden, width = weights[0].shape
    held = inputs[0]
    owners, whole, wide = held.shape
    count = owners * (whole + 1)
    block = jax.ShapeDtypeStruct(held.shape, bf16)
    kept = jax.ShapeDtypeStruct((count, hidden), f32)
    summed = jax.ShapeDtypeStruct((1, width), f32)
    out_shape = {"forward": [block, kept], "backward": [block, summed], "both": [block, block]}
    out_shape = out_shape[mode]
    vmem = pl.BlockSpec(memory_space=pltpu.VMEM)
    anywhere = pl.BlockSpec(memory_space=pl.ANY)
    steps = len(chunks(hidden, HIDDEN_STEP))
    n_mm = 4 if mode == "both" else 2
    return pl.pallas_call(
        functools.partial(expert_kernel, mode, layer),
        out_shape=out_shape,
        in_specs=[vmem] * len(inputs) + [anywhere] * 4,
        out_specs=[vmem] * len(out_shape),
        scratch_shapes=[
            pltpu.VMEM((hidden, width), bf16),
            pltpu.VMEM((hidden, width), bf16),
            pltpu.VMEM((count, width), bf16),
            pltpu.VMEM((count, hidden), f32),
            pltpu.VMEM((count, hidden), bf16),
            pltpu.VMEM((owners, whole, LANES), f32),
            pltpu.SemaphoreType.DMA((steps,)),
            pltpu.SemaphoreType.DMA((steps,)),
        ],
        compiler_params=pltpu.CompilerParams(vmem_limit_bytes=VMEM_BYTES),
        cost_estimate=pl.CostEstimate(
            flops=2 * n_mm * count * hidden * width,
            bytes_accessed=4 * hidden * width + 4 * count * width,
            transcendentals=count * hidden,
        ),
        name="expert_" + mode,
    )(*inputs, *weights)


def tables_kernel(top, whole, packed, plain, weighted):
    row_count, count = plain.shape
    owners = count // (whole + 1)
    main = owners * whole
    own_lane = lax.broadcasted_iota(jnp.int32, (row_count, owners), 1)
    hot = jnp.zeros((row_count, owners), f32)
    share = jnp.zeros((row_count, owners), f32)
    total = jnp.zeros((row_count, 1), f32)
    counts = packed[:, top : top + 1]
    for k in range(top):
        named = packed[:, k : k + 1] == own_lane
        fixed = packed[:, top + 1 + k : top + 2 + k].astype(f32)
        fixed = jnp.where(counts > k, fixed, 0.0)
        hot = hot + jnp.where(named, 1.0, 0.0)
        share = share + jnp.where(named, fixed, 0.0)
        total = total + fixed
    share = share / total
    owner = lax.broadcasted_iota(jnp.int32, (owners, count), 0)
    column = lax.broadcasted_iota(jnp.int32, (owners, count), 1)
    place = column - owner * whole
    inside = (place >= 0) & (place < whole) & (column < main)
    spread = jnp.where(inside | (column - main == owner), 1.0, 0.0)
    place = jnp.sum(jnp.where(inside, place, 0).astype(f32), axis=0, keepdims=True)
    last = lax.broadcasted_iota(jnp.int32, (1, count), 1) >= main
    place = jnp.where(last, float(whole), place)
    spread = spread.astype(bf16)
    row = lax.broadcasted_iota(jnp.int32, (row_count, row_count), 0)
    earlier = lax.broadcasted_iota(jnp.int32, (row_count, row_count), 1) < row
    below = jnp.where(earlier, 1.0, 0.0).astype(bf16)
    before = jnp.dot(below, hot.astype(bf16), preferred_element_type=f32)
    hot_c = jnp.dot(hot.astype(bf16), spread, preferred_element_type=f32)
    before_c = jnp.dot(before.astype(bf16), spread, preferred_element_type=f32)
    share_c = jnp.dot(share.astype(bf16), spread, preferred_element_type=f32)
    chosen = jnp.where(before_c == place, hot_c, 0.0)
    plain[...] = chosen.astype(bf16)
    weighted[...] = (chosen * share_c).astype(bf16)


def pallas(kernel, out_shape, scratch, name, *inputs, awaits=()):
    vmem = pl.BlockSpec(memory_space=pltpu.VMEM)

    def body(*refs):
        awaited, refs = refs[len(inputs) : len(inputs) + len(awaits)], (
            refs[: len(inputs)] + refs[len(inputs) + len(awaits) :]
        )
        if awaited:
            refs, (tile, sem) = refs[:-2], refs[-2:]
        for ref in awaited:
            copy = pltpu.make_async_copy(ref.at[pl.ds(0, 16), pl.ds(0, LANES)], tile, sem)
            copy.start()
            copy.wait()
        kernel(*refs)

    if awaits:
        scratch = [*scratch, pltpu.VMEM((16, LANES), bf16), pltpu.SemaphoreType.DMA(())]

    return pl.pallas_call(
        body,
        out_shape=out_shape,
        in_specs=[vmem] * len(inputs) + [pl.BlockSpec(memory_space=pl.ANY)] * len(awaits),
        out_specs=jax.tree.map(lambda _: vmem, out_shape),
        scratch_shapes=scratch,
        compiler_params=pltpu.CompilerParams(vmem_limit_bytes=VMEM_BYTES),
        name=name,
    )(*inputs, *awaits)


def pack(table, rows, out, tails):
    width = rows.shape[1]
    for s, n in chunks(width, WIDTH_STEP):
        value = lax.dot_general(
            table[...], rows[:, s : s + n], (((0,), (0,)), ((), ())), preferred_element_type=f32
        )
        store_columns(out, tails, s, value)
    store_tails(out, tails)


def normed(state_f):
    mean = jnp.mean(state_f * state_f, axis=-1, keepdims=True)
    inverse_rms = lax.rsqrt(mean + EPSILON)
    return state_f * inverse_rms, inverse_rms


def four(parts):
    own, far, left, right = (p[...].astype(f32) for p in parts)
    return (own + far) + (left + right)


def plain_kernel(rows, table, out, tails):
    pack(table, rows, out, tails)


def norm_kernel(x, gain, table, out, rows, tails):
    rows[...] = (normed(x[...].astype(f32))[0] * gain[...]).astype(bf16)
    pack(table, rows, out, tails)


def sum_norm_kernel(x, p0, p1, p2, p3, gain, table, following, out, rows, tails):
    following[...] = (x[...].astype(f32) + four((p0, p1, p2, p3))).astype(bf16)
    rows[...] = (normed(following[...].astype(f32))[0] * gain[...]).astype(bf16)
    pack(table, rows, out, tails)


def finish(x, upstream, parts, gain, grad, gain_grad=None):
    d_norm = four(parts)
    scaled, inverse_rms = normed(x[...].astype(f32))
    d_scaled = d_norm * gain[...]
    mean = jnp.mean(d_scaled * scaled, axis=-1, keepdims=True)
    d_input = inverse_rms * (d_scaled - scaled * mean)
    grad[...] = (upstream[...].astype(f32) + d_input).astype(bf16)
    if gain_grad is not None:
        gain_grad[...] = jnp.sum(d_norm * scaled, axis=0, keepdims=True)


def finish_kernel(x, upstream, p0, p1, p2, p3, gain, grad):
    finish(x, upstream, (p0, p1, p2, p3), gain, grad)


def finish_pack_kernel(x, upstream, p0, p1, p2, p3, gain, table, grad, gain_grad, out, tails):
    finish(x, upstream, (p0, p1, p2, p3), gain, grad, gain_grad)
    pack(table, grad, out, tails)


def home_kernel(table, held, out, tails):
    owners, whole, wide = held.shape
    width = wide - LANES
    main = owners * whole
    tails[...] = held[:, :, width:wide].astype(f32)
    for s, n in chunks(width, WIDTH_STEP):
        rows = held[:, :, s : s + n].reshape(main, n)
        last = [tails[:, (s // LANES) + c, :] for c in range(n // LANES)]
        last = jnp.concatenate(last, axis=1).astype(bf16)
        value = jnp.dot(table[:, :main], rows, preferred_element_type=f32)
        value = value + jnp.dot(table[:, main:], last, preferred_element_type=f32)
        out[:, s : s + n] = value.astype(bf16)


def swapped(x):
    return lax.ppermute(x, "section", SWAP)


def after(value, first_done):
    return lax.optimization_barrier((value, first_done))[0]


def shards(inputs, cotangent, gain, w_up, w_down, expert_ids, expert_counts, combine_fixed):
    section = lax.axis_index("section")
    owners = lax.axis_size("dp")
    ring = lax.axis_size("expert")
    row_count, width = inputs.shape[1:]
    top = expert_ids.shape[3]
    capacity = min(row_count, row_count * top // owners + 1)
    whole = capacity - 1
    count = owners * capacity
    first = section == 0
    up_own, down_own = w_up[0, 0], w_down[0, 0]

    def like(*shape, dtype=bf16):
        return jax.ShapeDtypeStruct(shape, dtype)

    block = like(owners, whole, width + LANES)
    rows_shape = like(row_count, width)
    gain_shape = like(1, width, dtype=f32)
    table_shape = like(row_count, count)
    tails = pltpu.VMEM((owners, whole, LANES), f32)
    rows = pltpu.VMEM((row_count, width), bf16)

    def pick(mine, other, layer):
        return jnp.where(section == layer, mine, other)

    ints = jnp.concatenate([expert_ids[0], expert_counts[0][..., None], combine_fixed[0]], axis=-1)
    mine = lax.dynamic_index_in_dim(ints, section, 0, keepdims=False)
    theirs = swapped(lax.dynamic_index_in_dim(ints, 1 - section, 0, keepdims=False))
    gain_own = gain.astype(f32)
    gain_other = swapped(gain_own)
    x0 = lax.dynamic_index_in_dim(inputs, section, 0, keepdims=False)
    upstream = lax.dynamic_index_in_dim(cotangent, section, 0, keepdims=False)
    up_other, down_other = swapped(up_own), swapped(down_own)

    def tables(packed):
        kernel = functools.partial(tables_kernel, top, whole)
        return pallas(kernel, [table_shape, table_shape], [], "tables", packed)

    def exchange(held):
        return lax.all_to_all(held, "dp", split_axis=0, concat_axis=0, tiled=True)

    def over_groups(part):
        pairs = [[(i, (i + by) % ring) for i in range(ring)] for by in (2, 1, 3)]
        return (part, *[lax.ppermute(part, "expert", p) for p in pairs])

    def home(table, held):
        return over_groups(pallas(home_kernel, rows_shape, [tails], "home", table, held))

    weights = (up_own, down_own, up_other, down_other)

    def enter(current, gain_row, table, *awaits):
        args = (current, gain_row, table)
        return exchange(pallas(norm_kernel, block, [rows, tails], "enter", *args, awaits=awaits))

    own_tables = tables(mine)
    rows0 = lax.cond(
        first,
        enter,
        lambda *a: jnp.zeros(block.shape, bf16),
        x0,
        gain_own,
        own_tables[0],
    )
    other_tables = tables(theirs)
    rows0 = lax.cond(
        first,
        lambda kept, *a: kept,
        lambda kept, *a: enter(*a),
        rows0,
        x0,
        gain_other,
        other_tables[0],
        up_other,
        down_other,
    )
    gain0, gain1 = (pick(gain_own, gain_other, layer) for layer in range(2))
    plain0, plain1 = (pick(own_tables[0], other_tables[0], layer) for layer in range(2))
    weighted0, weighted1 = (pick(own_tables[1], other_tables[1], layer) for layer in range(2))
    d_held1 = pallas(plain_kernel, block, [tails], "spread", upstream, weighted1)

    part0, pre0 = expert("forward", 0, weights, rows0)
    back0 = exchange(part0)
    d_rows1 = exchange(after(d_held1, back0))
    sums0 = home(weighted0, back0)
    x1, held1 = pallas(
        sum_norm_kernel, [rows_shape, block], [rows, tails], "next", x0, *sums0, gain1, plain1
    )
    rows1 = exchange(after(held1, d_rows1))
    part1, d_part1 = expert("both", 1, weights, rows1, d_rows1)
    d_back1 = exchange(d_part1)
    back1 = exchange(after(part1, d_back1))
    d_sums1 = home(plain1, d_back1)
    grad1, gain_grad1, d_held0 = pallas(
        finish_pack_kernel,
        [rows_shape, gain_shape, block],
        [tails],
        "finish_next",
        x1,
        upstream,
        *d_sums1,
        gain1,
        weighted0,
    )
    d_rows0 = exchange(after(d_held0, back1))
    d_part0, gain_part0 = expert("backward", 0, weights, d_rows0, pre0, rows0)
    x2 = (x1.astype(f32) + four(home(weighted1, back1))).astype(bf16)
    d_back0 = exchange(d_part0)

    gain_part0 = gain_part0 / gain0
    gain_part1 = jnp.where(lax.axis_index("expert") == 0, gain_grad1, 0.0)
    slices = jnp.stack([gain_part0, gain_part1]).reshape(2, owners, width // owners)
    slices = jnp.broadcast_to(slices.transpose(1, 0, 2)[:, None], (owners, ring, 2, width // owners))
    slices = after(slices, d_back0).reshape(owners * ring, 2, width // owners)
    slices = lax.all_to_all(slices, ("dp", "expert"), split_axis=0, concat_axis=0, tiled=True)
    slices = jnp.sum(slices, axis=0)

    grad0 = pallas(finish_kernel, rows_shape, [], "finish", x0, grad1, *home(plain0, d_back0), gain0)

    gain_sum = pick(slices[0], slices[1], 0) + swapped(pick(slices[1], slices[0], 0))
    kept_x, taken_x = pick(x1, x2, 0), swapped(pick(x2, x1, 0))
    kept_g, taken_g = pick(grad0, grad1, 0), swapped(pick(grad1, grad0, 0))

    def both(kept, taken):
        low, high = jnp.where(first, kept, taken), jnp.where(first, taken, kept)
        return jnp.stack([low, high])[None]

    return both(kept_x, taken_x), both(kept_g, taken_g), gain_sum[None]


def solution(mesh):
    return jax.shard_map(
        shards,
        mesh=mesh,
        in_specs=(
            P(None, "dp", None),
            P(None, "dp", None),
            P("section", None),
            P("section", "dp", "expert", None),
            P("section", "dp", "expert", None),
            P("section", None, "dp", None),
            P("section", None, "dp"),
            P("section", None, "dp", None),
        ),
        out_specs=(
            P("section", None, "dp", None),
            P("section", None, "dp", None),
            P("section", "dp"),
        ),
        check_vma=False,
    )
```

```python
import functools

import jax
import jax.numpy as jnp
from jax import lax
from jax.experimental import pallas as pl
from jax.experimental.pallas import tpu as pltpu
from jax.sharding import PartitionSpec as P

EPSILON = 1e-05
SWAP = [(0, 1), (1, 0)]
LANES = 128
HIDDEN_STEP = 256
COPY_STEP = 224
WIDTH_STEP = 512
VMEM_BYTES = 48 * 1024 * 1024
bf16, f32 = jnp.bfloat16, jnp.float32


def over_columns(width, body, unrolled=False):
    if unrolled:
        for i in range(width // WIDTH_STEP):
            body(i, i * WIDTH_STEP, WIDTH_STEP)
        return

    @pl.loop(0, width // WIDTH_STEP)
    def _(i):
        body(i, pl.multiple_of(i * WIDTH_STEP, WIDTH_STEP), WIDTH_STEP)


def load_rows(held, rows, tails):
    owners, whole, _ = held.shape
    width = rows.shape[1]
    main = owners * whole

    def load(i, s, n):
        rows[0:main, pl.ds(s, n)] = held[:, :, pl.ds(s, n)].reshape(main, n)

    over_columns(width, load)
    tails[...] = held[:, :, width : width + LANES].astype(f32)
    for c in range(width // LANES):
        rows[main : main + owners, c * LANES : (c + 1) * LANES] = tails[:, c, :].astype(bf16)


def store_columns(out, by_lane, i, start, value):
    owners, whole, _ = out.shape
    main = owners * whole
    size = value.shape[1]
    out[:, :, pl.ds(start, size)] = value[:main].astype(bf16).reshape(owners, whole, size)
    for c in range(size // LANES):
        by_lane[i * (size // LANES) + c] = value[main:, c * LANES : (c + 1) * LANES]


def store_tails(out, by_lane, tails, width):
    for c in range(by_lane.shape[0]):
        tails[:, c, :] = by_lane[c]
    out[:, :, width : width + LANES] = tails[...].astype(bf16)


def store_gain(out, gain_cols, width):
    value = jnp.broadcast_to(gain_cols[...][None], (out.shape[0], *gain_cols.shape))
    out[:, :, width + LANES : width + 2 * LANES] = value.astype(bf16)


def sum_gain(held, width):
    return jnp.sum(held[:, :, width + LANES : width + 2 * LANES].astype(f32), axis=0)


def by_units(rows, weights):
    return lax.dot_general(rows, weights, (((1,), (1,)), ((), ())), preferred_element_type=f32)


def sigmoid(v):
    return 1.0 / (1.0 + jnp.exp(-v))


def expert_kernel(mode, layer, n_in, n_out, n_held, *refs):
    ins, refs = refs[:n_in], refs[n_in:]
    own_hbm, other_hbm, refs = refs[:2], refs[2:4], refs[4:]
    outs, refs = refs[:n_out], refs[n_out:]
    up, down, rows, act, tails, by_lane, up_sem, down_sem, in_sem, out_sem, *refs = refs
    held, refs = refs[:n_held], refs[n_held:]
    hidden, width = up.shape
    loops, columns = hidden // HIDDEN_STEP, width // WIDTH_STEP
    rest = hidden - loops * HIDDEN_STEP
    backward = mode == "backward"

    arrivals = [
        pltpu.make_async_copy(src, dst, in_sem.at[i]) for i, (src, dst) in enumerate(zip(ins, held))
    ]
    for copy in arrivals:
        copy.start()

    def copy_of(k, i, pair):
        part = pl.ds(pl.multiple_of(i * COPY_STEP, COPY_STEP), COPY_STEP)
        dst, sem = ((up, up_sem), (down, down_sem))[k]
        return pltpu.make_async_copy(pair[k].at[part, :], dst.at[part, :], sem.at[i])

    def start(pair):
        for k in (1, 0) if backward else (0, 1):

            @pl.loop(0, hidden // COPY_STEP)
            def _(i):
                copy_of(k, i, pair).start()

    mine = lax.axis_index("section") == layer
    pl.when(mine)(lambda: start(own_hbm))
    pl.when(jnp.logical_not(mine))(lambda: start(other_hbm))

    def hidden_units(weights, body, k=None):
        if k is not None:
            copy_of(k, 0, own_hbm).wait()

        @pl.loop(0, loops)
        def _(i):
            if k is not None:
                copy_of(k, i + 1, own_hbm).wait()
            at = pl.ds(pl.multiple_of(i * HIDDEN_STEP, HIDDEN_STEP), HIDDEN_STEP)
            body(at, by_units(rows[...], weights[at, :]))

        at = pl.ds(loops * HIDDEN_STEP, rest)
        body(at, by_units(rows[...], weights[at, :]))

    def gradient(pre):
        def body(at, v):
            p = pre[:, at].astype(f32)
            g = sigmoid(p)
            act[:, at] = (v * g * (1.0 + p * (1.0 - g))).astype(bf16)

        return body

    def activation(pre):
        def body(at, v):
            pre[:, at] = v.astype(pre.dtype)
            act[:, at] = (v * sigmoid(v)).astype(bf16)

        return body

    def leave(stage, out, number, s, n):
        part = (slice(None), slice(None), pl.ds(s, n))
        return pltpu.make_async_copy(stage.at[part], out.at[part], out_sem.at[number])

    def results(weights, stage, out, number, gain_cols=None):
        def step(i, s, n):
            value = jnp.dot(act[...], weights[:, pl.ds(s, n)], preferred_element_type=f32)
            store_columns(stage, by_lane, i, s, value)
            leave(stage, out, number + i, s, n).start()
            if gain_cols is not None:
                terms = value * rows[:, pl.ds(s, n)].astype(f32)
                summed = jnp.sum(terms, axis=0, keepdims=True)
                for c in range(n // LANES):
                    at = pl.ds(i * (n // LANES) + c, 1)
                    gain_cols[at, :] = summed[:, c * LANES : (c + 1) * LANES]

        over_columns(width, step)
        store_tails(stage, by_lane, tails, width)
        if gain_cols is not None:
            store_gain(stage, gain_cols, width)
        leave(stage, out, number + columns, width, stage.shape[2] - width).start()

    def left(stage, out, number):
        over_columns(width, lambda i, s, n: leave(stage, out, number + i, s, n).wait())
        leave(stage, out, number + columns, width, stage.shape[2] - width).wait()

    def all_here(k):
        @pl.loop(0, hidden // COPY_STEP)
        def _(i):
            copy_of(k, i, own_hbm).wait()

    arrivals[0].wait()
    load_rows(held[0], rows, tails)
    if backward:
        stage, gain_cols, tile = refs
        arrivals[1].wait()
        hidden_units(down, gradient(held[1]), 1)
        outs[1][...] = sum_gain(held[0], width)
        arrivals[2].wait()
        load_rows(held[2], rows, tails)
        copy = pltpu.make_async_copy(ins[3].at[pl.ds(0, 16), pl.ds(0, LANES)], tile, in_sem.at[3])
        copy.start()
        copy.wait()
        all_here(0)
        results(up, stage, outs[0], 0, gain_cols)
        left(stage, outs[0], 0)
        return
    stage, pre, *refs = refs
    hidden_units(up, activation(pre), 0)
    all_here(1)
    if mode == "forward":
        kept = pltpu.make_async_copy(pre, outs[1], in_sem.at[1])
        kept.start()
        results(down, stage, outs[0], 0)
        kept.wait()
    else:
        (d_stage,) = refs
        results(down, stage, outs[0], 0)
        arrivals[1].wait()
        load_rows(held[1], rows, tails)
        hidden_units(down, gradient(pre))
        results(up, d_stage, outs[1], columns + 1)
        left(d_stage, outs[1], columns + 1)
    left(stage, outs[0], 0)


def expert(mode, layer, weights, *inputs):
    hidden, width = weights[0].shape
    owners, whole, wide = inputs[0].shape
    count = owners * (whole + 1)
    copies, columns = hidden // COPY_STEP, width // WIDTH_STEP
    block = jax.ShapeDtypeStruct((owners, whole, wide), bf16)
    pre = jax.ShapeDtypeStruct((count, hidden), bf16)
    cols = jax.ShapeDtypeStruct((width // LANES, LANES), f32)
    out_shape = {"forward": [block, pre], "backward": [block, cols], "both": [block, block]}[mode]
    stage = pltpu.VMEM(block.shape, bf16)
    held = [pltpu.VMEM(x.shape, x.dtype) for x in inputs[:3]]
    own_scratch = {
        "forward": [stage, pltpu.VMEM(pre.shape, bf16)],
        "backward": [stage, pltpu.VMEM(cols.shape, f32), pltpu.VMEM((16, LANES), bf16)],
        "both": [stage, pltpu.VMEM(pre.shape, f32), stage],
    }[mode]
    in_hbm = pl.BlockSpec(memory_space=pltpu.HBM)
    anywhere = pl.BlockSpec(memory_space=pl.ANY)
    vmem = pl.BlockSpec(memory_space=pltpu.VMEM)
    n_mm = 4 if mode == "both" else 2
    return pl.pallas_call(
        functools.partial(expert_kernel, mode, layer, len(inputs), 2, len(held)),
        out_shape=out_shape,
        in_specs=[anywhere] * (len(inputs) + 4),
        out_specs=[in_hbm, vmem if mode == "backward" else in_hbm],
        scratch_shapes=[
            pltpu.VMEM((hidden, width), bf16),
            pltpu.VMEM((hidden, width), bf16),
            pltpu.VMEM((count, width), bf16),
            pltpu.VMEM((count, hidden), bf16),
            pltpu.VMEM((owners, whole, LANES), f32),
            pltpu.VMEM((width // LANES, owners, LANES), f32),
            pltpu.SemaphoreType.DMA((copies,)),
            pltpu.SemaphoreType.DMA((copies,)),
            pltpu.SemaphoreType.DMA((4,)),
            pltpu.SemaphoreType.DMA((2 * columns + 2,)),
            *held,
            *own_scratch,
        ],
        compiler_params=pltpu.CompilerParams(vmem_limit_bytes=VMEM_BYTES),
        cost_estimate=pl.CostEstimate(
            flops=2 * n_mm * count * hidden * width,
            bytes_accessed=4 * hidden * width + 4 * count * width,
            transcendentals=count * hidden,
        ),
        name="expert_" + mode,
    )(*inputs, *weights)


def tables_kernel(top, whole, packed, plain, weighted):
    row_count, count = plain.shape
    owners = count // (whole + 1)
    main = owners * whole
    own_lane = lax.broadcasted_iota(jnp.int32, (row_count, owners), 1)
    hot = jnp.zeros((row_count, owners), f32)
    share = jnp.zeros((row_count, owners), f32)
    total = jnp.zeros((row_count, 1), f32)
    counts = packed[:, top : top + 1]
    for k in range(top):
        named = packed[:, k : k + 1] == own_lane
        fixed = packed[:, top + 1 + k : top + 2 + k].astype(f32)
        fixed = jnp.where(counts > k, fixed, 0.0)
        hot = hot + jnp.where(named, 1.0, 0.0)
        share = share + jnp.where(named, fixed, 0.0)
        total = total + fixed
    share = share / total
    owner = lax.broadcasted_iota(jnp.int32, (owners, count), 0)
    column = lax.broadcasted_iota(jnp.int32, (owners, count), 1)
    place = column - owner * whole
    inside = (place >= 0) & (place < whole) & (column < main)
    spread = jnp.where(inside | (column - main == owner), 1.0, 0.0)
    place = jnp.sum(jnp.where(inside, place, 0).astype(f32), axis=0, keepdims=True)
    last = lax.broadcasted_iota(jnp.int32, (1, count), 1) >= main
    place = jnp.where(last, float(whole), place)
    spread = spread.astype(bf16)
    row = lax.broadcasted_iota(jnp.int32, (row_count, row_count), 0)
    earlier = lax.broadcasted_iota(jnp.int32, (row_count, row_count), 1) < row
    below = jnp.where(earlier, 1.0, 0.0).astype(bf16)
    before = jnp.dot(below, hot.astype(bf16), preferred_element_type=f32)
    hot_c = jnp.dot(hot.astype(bf16), spread, preferred_element_type=f32)
    before_c = jnp.dot(before.astype(bf16), spread, preferred_element_type=f32)
    share_c = jnp.dot(share.astype(bf16), spread, preferred_element_type=f32)
    chosen = jnp.where(before_c == place, hot_c, 0.0)
    plain[...] = chosen.astype(bf16)
    weighted[...] = (chosen * share_c).astype(bf16)


def pallas(kernel, out_shape, scratch, name, *inputs, awaits=()):
    vmem = pl.BlockSpec(memory_space=pltpu.VMEM)

    def body(*refs):
        awaited, refs = refs[len(inputs) : len(inputs) + len(awaits)], (
            refs[: len(inputs)] + refs[len(inputs) + len(awaits) :]
        )
        if awaited:
            refs, (tile, sem) = refs[:-2], refs[-2:]
        for ref in awaited:
            part = (0,) * (len(ref.shape) - 2) + (pl.ds(0, 16), pl.ds(0, LANES))
            copy = pltpu.make_async_copy(ref.at[part], tile, sem)
            copy.start()
            copy.wait()
        kernel(*refs)

    if awaits:
        scratch = [*scratch, pltpu.VMEM((16, LANES), bf16), pltpu.SemaphoreType.DMA(())]

    return pl.pallas_call(
        body,
        out_shape=out_shape,
        in_specs=[vmem] * len(inputs) + [pl.BlockSpec(memory_space=pl.ANY)] * len(awaits),
        out_specs=jax.tree.map(lambda _: vmem, out_shape),
        scratch_shapes=scratch,
        compiler_params=pltpu.CompilerParams(vmem_limit_bytes=VMEM_BYTES),
        name=name,
    )(*inputs, *awaits)


def pack(table, rows, out, by_lane, tails):
    width = rows.shape[1]

    def step(i, s, n):
        value = lax.dot_general(
            table[...], rows[:, pl.ds(s, n)], (((0,), (0,)), ((), ())), preferred_element_type=f32
        )
        store_columns(out, by_lane, i, s, value)

    over_columns(width, step, unrolled=True)
    store_tails(out, by_lane, tails, width)


def normed(state_f):
    mean = jnp.mean(state_f * state_f, axis=-1, keepdims=True)
    inverse_rms = lax.rsqrt(mean + EPSILON)
    return state_f * inverse_rms, inverse_rms


def four(parts):
    own, far, left, right = (p[...].astype(f32) for p in parts)
    return (own + far) + (left + right)


def plain_kernel(rows, table, out, *tails):
    pack(table, rows, out, *tails)


def norm_kernel(x, gain, table, out, rows, *tails):
    rows[...] = (normed(x[...].astype(f32))[0] * gain[...]).astype(bf16)
    pack(table, rows, out, *tails)


def sum_norm_kernel(x, p0, p1, p2, p3, gain, table, following, out, rows, *tails):
    following[...] = (x[...].astype(f32) + four((p0, p1, p2, p3))).astype(bf16)
    rows[...] = (normed(following[...].astype(f32))[0] * gain[...]).astype(bf16)
    pack(table, rows, out, *tails)


def finish(x, upstream, parts, gain, grad):
    d_norm = four(parts)
    scaled, inverse_rms = normed(x[...].astype(f32))
    d_scaled = d_norm * gain[...]
    mean = jnp.mean(d_scaled * scaled, axis=-1, keepdims=True)
    d_input = inverse_rms * (d_scaled - scaled * mean)
    grad[...] = (upstream[...].astype(f32) + d_input).astype(bf16)
    return jnp.sum(d_norm * scaled, axis=0, keepdims=True)


def finish_kernel(x, upstream, p0, p1, p2, p3, gain, grad):
    finish(x, upstream, (p0, p1, p2, p3), gain, grad)


def finish_pack_kernel(x, upstream, p0, p1, p2, p3, gain, table, grad, out, gain_cols, *tails):
    gain_grad = finish(x, upstream, (p0, p1, p2, p3), gain, grad)
    for c in range(gain_cols.shape[0]):
        gain_cols[c : c + 1, :] = gain_grad[:, c * LANES : (c + 1) * LANES]
    pack(table, grad, out, *tails)
    store_gain(out, gain_cols, grad.shape[1])


def home_kernel(table, held, out, *refs):
    *summed, by_lane, tails = refs
    owners, whole, _ = held.shape
    width = out.shape[1]
    main = owners * whole
    tails[...] = held[:, :, width : width + LANES].astype(f32)
    for c in range(width // LANES):
        by_lane[c] = tails[:, c, :]

    def step(i, s, n):
        rows = held[:, :, pl.ds(s, n)].reshape(main, n)
        last = [by_lane[i * (n // LANES) + c] for c in range(n // LANES)]
        last = jnp.concatenate(last, axis=1).astype(bf16)
        value = jnp.dot(table[:, :main], rows, preferred_element_type=f32)
        value = value + jnp.dot(table[:, main:], last, preferred_element_type=f32)
        out[:, pl.ds(s, n)] = value.astype(bf16)

    over_columns(width, step, unrolled=True)
    for ref in summed:
        ref[...] = sum_gain(held, width)


def swapped(x):
    return lax.ppermute(x, "section", SWAP)


def after(value, first_done):
    return lax.optimization_barrier((value, first_done))[0]


def shards(inputs, cotangent, gain, w_up, w_down, expert_ids, expert_counts, combine_fixed):
    section = lax.axis_index("section")
    owners = lax.axis_size("dp")
    ring = lax.axis_size("expert")
    row_count, width = inputs.shape[1:]
    top = expert_ids.shape[3]
    capacity = min(row_count, row_count * top // owners + 1)
    whole = capacity - 1
    count = owners * capacity
    first = section == 0
    up_own, down_own = w_up[0, 0], w_down[0, 0]

    def like(*shape, dtype=bf16):
        return jax.ShapeDtypeStruct(shape, dtype)

    block = like(owners, whole, width + LANES)
    gain_block = like(owners, whole, width + 2 * LANES)
    cols_shape = like(width // LANES, LANES, dtype=f32)
    rows_shape = like(row_count, width)
    table_shape = like(row_count, count)
    tails = [
        pltpu.VMEM((width // LANES, owners, LANES), f32),
        pltpu.VMEM((owners, whole, LANES), f32),
    ]
    rows = pltpu.VMEM((row_count, width), bf16)

    def pick(mine, other, layer):
        return jnp.where(section == layer, mine, other)

    ints = jnp.concatenate([expert_ids[0], expert_counts[0][..., None], combine_fixed[0]], axis=-1)
    mine = lax.dynamic_index_in_dim(ints, section, 0, keepdims=False)
    theirs = swapped(lax.dynamic_index_in_dim(ints, 1 - section, 0, keepdims=False))
    gain_own = gain.astype(f32)
    gain_other = swapped(gain_own)
    x0 = lax.dynamic_index_in_dim(inputs, section, 0, keepdims=False)
    upstream = lax.dynamic_index_in_dim(cotangent, section, 0, keepdims=False)
    up_other, down_other = swapped(up_own), swapped(down_own)

    def tables(packed, *awaits):
        kernel = functools.partial(tables_kernel, top, whole)
        return pallas(kernel, [table_shape, table_shape], [], "tables", packed, awaits=awaits)

    def exchange(held):
        return lax.all_to_all(held, "dp", split_axis=0, concat_axis=0, tiled=True)

    def over_groups(part):
        pairs = [[(i, (i + by) % ring) for i in range(ring)] for by in (2, 1, 3)]
        return (part, *[lax.ppermute(part, "expert", p) for p in pairs])

    def home(table, held):
        return over_groups(pallas(home_kernel, [rows_shape], tails, "home", table, held)[0])

    weights = (up_own, down_own, up_other, down_other)

    def enter(current, gain_row, table, *awaits):
        args = (current, gain_row, table)
        return exchange(pallas(norm_kernel, block, [rows, *tails], "enter", *args, awaits=awaits))

    own_tables = tables(mine)
    rows0 = lax.cond(
        first,
        enter,
        lambda *a: jnp.zeros(block.shape, bf16),
        x0,
        gain_own,
        own_tables[0],
    )
    other_tables = tables(theirs, rows0)
    rows0 = lax.cond(
        first,
        lambda kept, *a: kept,
        lambda kept, *a: enter(*a),
        rows0,
        x0,
        gain_other,
        other_tables[0],
        up_other,
        down_other,
    )
    gain0, gain1 = (pick(gain_own, gain_other, layer) for layer in range(2))
    plain0, plain1 = (pick(own_tables[0], other_tables[0], layer) for layer in range(2))
    weighted0, weighted1 = (pick(own_tables[1], other_tables[1], layer) for layer in range(2))
    d_held1 = pallas(plain_kernel, block, tails, "spread", upstream, weighted1)

    part0, pre0 = expert("forward", 0, weights, rows0)
    back0 = exchange(part0)
    d_rows1 = exchange(after(d_held1, back0))
    sums0 = home(weighted0, back0)
    x1, held1 = pallas(
        sum_norm_kernel, [rows_shape, block], [rows, *tails], "next", x0, *sums0, gain1, plain1
    )
    rows1 = exchange(after(held1, d_rows1))
    part1, d_part1 = expert("both", 1, weights, rows1, d_rows1)
    d_back1 = exchange(d_part1)
    back1 = exchange(after(part1, d_back1))
    d_sums1 = home(plain1, d_back1)
    grad1, d_held0 = pallas(
        finish_pack_kernel,
        [rows_shape, gain_block],
        [pltpu.VMEM(cols_shape.shape, f32), *tails],
        "finish_next",
        x1,
        upstream,
        *d_sums1,
        gain1,
        weighted0,
    )
    d_rows0 = exchange(after(d_held0, back1))
    x2 = (x1.astype(f32) + four(home(weighted1, back1))).astype(bf16)
    d_part0, gain_sum1 = expert("backward", 0, weights, d_rows0, pre0, rows0, x2)
    d_back0 = exchange(d_part0)
    kept_x, taken_x = pick(x1, x2, 0), swapped(pick(x2, x1, 0))
    d_home0, gain_sum0 = pallas(
        home_kernel,
        [rows_shape, cols_shape],
        tails,
        "home_gain",
        plain0,
        d_back0,
        awaits=(taken_x,),
    )
    d_sums0 = over_groups(d_home0)
    gain_sum0 = four(over_groups(gain_sum0)) / gain0.reshape(cols_shape.shape)
    grad0 = pallas(finish_kernel, rows_shape, [], "finish", x0, grad1, *d_sums0, gain0)

    kept_g, taken_g = pick(grad0, grad1, 0), swapped(pick(grad1, grad0, 0))

    def gain_slice(summed):
        summed = summed.reshape(owners, width // owners)
        return lax.dynamic_index_in_dim(summed, lax.axis_index("dp"), 0, keepdims=False)

    slice0, slice1 = gain_slice(gain_sum0), gain_slice(gain_sum1)
    gain_sum = pick(slice0, slice1, 0) + swapped(pick(slice1, slice0, 0))

    def both(kept, taken):
        low, high = jnp.where(first, kept, taken), jnp.where(first, taken, kept)
        return jnp.stack([low, high])[None]

    return both(kept_x, taken_x), both(kept_g, taken_g), gain_sum[None]


def solution(mesh):
    return jax.shard_map(
        shards,
        mesh=mesh,
        in_specs=(
            P(None, "dp", None),
            P(None, "dp", None),
            P("section", None),
            P("section", "dp", "expert", None),
            P("section", "dp", "expert", None),
            P("section", None, "dp", None),
            P("section", None, "dp"),
            P("section", None, "dp", None),
        ),
        out_specs=(
            P("section", None, "dp", None),
            P("section", None, "dp", None),
            P("section", "dp"),
        ),
        check_vma=False,
    )
```

```python
import functools

import jax
import jax.numpy as jnp
from jax import lax
from jax.experimental import pallas as pl
from jax.experimental.pallas import tpu as pltpu
from jax.sharding import PartitionSpec as P

EPSILON = 1e-05
SWAP = [(0, 1), (1, 0)]
LANES = 128
HIDDEN_STEP = 256
COPY_STEP = 224
WIDTH_STEP = 512
VMEM_BYTES = 48 * 1024 * 1024
bf16, f32 = jnp.bfloat16, jnp.float32


def over_columns(width, body, unrolled=False):
    if unrolled:
        for i in range(width // WIDTH_STEP):
            body(i, i * WIDTH_STEP, WIDTH_STEP)
        return

    @pl.loop(0, width // WIDTH_STEP)
    def _(i):
        body(i, pl.multiple_of(i * WIDTH_STEP, WIDTH_STEP), WIDTH_STEP)


def load_rows(held, rows, tails):
    owners, whole, _ = held.shape
    width = rows.shape[1]
    main = owners * whole

    def load(i, s, n):
        rows[0:main, pl.ds(s, n)] = held[:, :, pl.ds(s, n)].reshape(main, n)

    over_columns(width, load)
    tails[...] = held[:, :, width : width + LANES].astype(f32)
    for c in range(width // LANES):
        rows[main : main + owners, c * LANES : (c + 1) * LANES] = tails[:, c, :].astype(bf16)


def store_columns(out, by_lane, i, start, value):
    owners, whole, _ = out.shape
    main = owners * whole
    size = value.shape[1]
    out[:, :, pl.ds(start, size)] = value[:main].astype(bf16).reshape(owners, whole, size)
    for c in range(size // LANES):
        by_lane[i * (size // LANES) + c] = value[main:, c * LANES : (c + 1) * LANES]


def store_tails(out, by_lane, tails, width):
    for c in range(by_lane.shape[0]):
        tails[:, c, :] = by_lane[c]
    out[:, :, width : width + LANES] = tails[...].astype(bf16)


def store_gain(out, gain_cols, width):
    value = jnp.broadcast_to(gain_cols[...][None], (out.shape[0], *gain_cols.shape))
    out[:, :, width + LANES : width + 2 * LANES] = value.astype(bf16)


def sum_gain(held, width):
    return jnp.sum(held[:, :, width + LANES : width + 2 * LANES].astype(f32), axis=0)


def by_units(rows, weights):
    return lax.dot_general(rows, weights, (((1,), (1,)), ((), ())), preferred_element_type=f32)


def sigmoid(v):
    return 1.0 / (1.0 + jnp.exp(-v))


def expert_kernel(mode, layer, n_in, n_out, n_held, *refs):
    ins, refs = refs[:n_in], refs[n_in:]
    own_hbm, other_hbm, refs = refs[:2], refs[2:4], refs[4:]
    outs, refs = refs[:n_out], refs[n_out:]
    up, down, rows, act, tails, by_lane, up_sem, down_sem, in_sem, out_sem, *refs = refs
    held, refs = refs[:n_held], refs[n_held:]
    hidden, width = up.shape
    loops, columns = hidden // HIDDEN_STEP, width // WIDTH_STEP
    rest = hidden - loops * HIDDEN_STEP
    backward = mode == "backward"

    arrivals = [
        pltpu.make_async_copy(src, dst, in_sem.at[i]) for i, (src, dst) in enumerate(zip(ins, held))
    ]
    for copy in arrivals:
        copy.start()

    def copy_of(k, i, pair):
        part = pl.ds(pl.multiple_of(i * COPY_STEP, COPY_STEP), COPY_STEP)
        dst, sem = ((up, up_sem), (down, down_sem))[k]
        return pltpu.make_async_copy(pair[k].at[part, :], dst.at[part, :], sem.at[i])

    def start(pair):
        for k in (1, 0) if backward else (0, 1):

            @pl.loop(0, hidden // COPY_STEP)
            def _(i):
                copy_of(k, i, pair).start()

    mine = lax.axis_index("section") == layer
    pl.when(mine)(lambda: start(own_hbm))
    pl.when(jnp.logical_not(mine))(lambda: start(other_hbm))

    def hidden_units(weights, body, k=None):
        if k is not None:
            copy_of(k, 0, own_hbm).wait()

        @pl.loop(0, loops)
        def _(i):
            if k is not None:
                copy_of(k, i + 1, own_hbm).wait()
            at = pl.ds(pl.multiple_of(i * HIDDEN_STEP, HIDDEN_STEP), HIDDEN_STEP)
            body(at, by_units(rows[...], weights[at, :]))

        at = pl.ds(loops * HIDDEN_STEP, rest)
        body(at, by_units(rows[...], weights[at, :]))

    def gradient(pre):
        def body(at, v):
            p = pre[:, at].astype(f32)
            g = sigmoid(p)
            act[:, at] = (v * g * (1.0 + p * (1.0 - g))).astype(bf16)

        return body

    def activation(pre):
        def body(at, v):
            pre[:, at] = v.astype(pre.dtype)
            act[:, at] = (v * sigmoid(v)).astype(bf16)

        return body

    def leave(stage, out, number, s, n):
        part = (slice(None), slice(None), pl.ds(s, n))
        return pltpu.make_async_copy(stage.at[part], out.at[part], out_sem.at[number])

    def results(weights, stage, out, number, gain_cols=None):
        def step(i, s, n):
            value = jnp.dot(act[...], weights[:, pl.ds(s, n)], preferred_element_type=f32)
            store_columns(stage, by_lane, i, s, value)
            leave(stage, out, number + i, s, n).start()
            if gain_cols is not None:
                terms = value * rows[:, pl.ds(s, n)].astype(f32)
                summed = jnp.sum(terms, axis=0, keepdims=True)
                for c in range(n // LANES):
                    at = pl.ds(i * (n // LANES) + c, 1)
                    gain_cols[at, :] = summed[:, c * LANES : (c + 1) * LANES]

        over_columns(width, step)
        store_tails(stage, by_lane, tails, width)
        if gain_cols is not None:
            store_gain(stage, gain_cols, width)
        leave(stage, out, number + columns, width, stage.shape[2] - width).start()

    def left(stage, out, number):
        over_columns(width, lambda i, s, n: leave(stage, out, number + i, s, n).wait())
        leave(stage, out, number + columns, width, stage.shape[2] - width).wait()

    def all_here(k):
        @pl.loop(0, hidden // COPY_STEP)
        def _(i):
            copy_of(k, i, own_hbm).wait()

    arrivals[0].wait()
    load_rows(held[0], rows, tails)
    if backward:
        stage, gain_cols, tile = refs
        arrivals[1].wait()
        hidden_units(down, gradient(held[1]), 1)
        outs[1][...] = sum_gain(held[0], width)
        arrivals[2].wait()
        load_rows(held[2], rows, tails)
        copy = pltpu.make_async_copy(ins[3].at[pl.ds(0, 16), pl.ds(0, LANES)], tile, in_sem.at[3])
        copy.start()
        copy.wait()
        all_here(0)
        results(up, stage, outs[0], 0, gain_cols)
        left(stage, outs[0], 0)
        return
    stage, pre, *refs = refs
    hidden_units(up, activation(pre), 0)
    all_here(1)
    if mode == "forward":
        kept = pltpu.make_async_copy(pre, outs[1], in_sem.at[1])
        kept.start()
        results(down, stage, outs[0], 0)
        kept.wait()
    else:
        (d_stage,) = refs
        results(down, stage, outs[0], 0)
        arrivals[1].wait()
        load_rows(held[1], rows, tails)
        hidden_units(down, gradient(pre))
        results(up, d_stage, outs[1], columns + 1)
        left(d_stage, outs[1], columns + 1)
    left(stage, outs[0], 0)


def expert(mode, layer, weights, *inputs):
    hidden, width = weights[0].shape
    owners, whole, wide = inputs[0].shape
    count = owners * (whole + 1)
    copies, columns = hidden // COPY_STEP, width // WIDTH_STEP
    block = jax.ShapeDtypeStruct((owners, whole, wide), bf16)
    pre = jax.ShapeDtypeStruct((count, hidden), bf16)
    cols = jax.ShapeDtypeStruct((width // LANES, LANES), f32)
    out_shape = {"forward": [block, pre], "backward": [block, cols], "both": [block, block]}[mode]
    stage = pltpu.VMEM(block.shape, bf16)
    held = [pltpu.VMEM(x.shape, x.dtype) for x in inputs[:3]]
    own_scratch = {
        "forward": [stage, pltpu.VMEM(pre.shape, bf16)],
        "backward": [stage, pltpu.VMEM(cols.shape, f32), pltpu.VMEM((16, LANES), bf16)],
        "both": [stage, pltpu.VMEM(pre.shape, f32), stage],
    }[mode]
    in_hbm = pl.BlockSpec(memory_space=pltpu.HBM)
    anywhere = pl.BlockSpec(memory_space=pl.ANY)
    vmem = pl.BlockSpec(memory_space=pltpu.VMEM)
    n_mm = 4 if mode == "both" else 2
    return pl.pallas_call(
        functools.partial(expert_kernel, mode, layer, len(inputs), 2, len(held)),
        out_shape=out_shape,
        in_specs=[anywhere] * (len(inputs) + 4),
        out_specs=[in_hbm, vmem if mode == "backward" else in_hbm],
        scratch_shapes=[
            pltpu.VMEM((hidden, width), bf16),
            pltpu.VMEM((hidden, width), bf16),
            pltpu.VMEM((count, width), bf16),
            pltpu.VMEM((count, hidden), bf16),
            pltpu.VMEM((owners, whole, LANES), f32),
            pltpu.VMEM((width // LANES, owners, LANES), f32),
            pltpu.SemaphoreType.DMA((copies,)),
            pltpu.SemaphoreType.DMA((copies,)),
            pltpu.SemaphoreType.DMA((4,)),
            pltpu.SemaphoreType.DMA((2 * columns + 2,)),
            *held,
            *own_scratch,
        ],
        compiler_params=pltpu.CompilerParams(vmem_limit_bytes=VMEM_BYTES),
        cost_estimate=pl.CostEstimate(
            flops=2 * n_mm * count * hidden * width,
            bytes_accessed=4 * hidden * width + 4 * count * width,
            transcendentals=count * hidden,
        ),
        name="expert_" + mode,
    )(*inputs, *weights)


def tables_kernel(top, whole, packed, plain, weighted):
    row_count, count = plain.shape
    owners = count // (whole + 1)
    main = owners * whole
    own_lane = lax.broadcasted_iota(jnp.int32, (row_count, owners), 1)
    hot = jnp.zeros((row_count, owners), f32)
    share = jnp.zeros((row_count, owners), f32)
    total = jnp.zeros((row_count, 1), f32)
    counts = packed[:, top : top + 1]
    for k in range(top):
        named = packed[:, k : k + 1] == own_lane
        fixed = packed[:, top + 1 + k : top + 2 + k].astype(f32)
        fixed = jnp.where(counts > k, fixed, 0.0)
        hot = hot + jnp.where(named, 1.0, 0.0)
        share = share + jnp.where(named, fixed, 0.0)
        total = total + fixed
    share = share / total
    owner = lax.broadcasted_iota(jnp.int32, (owners, count), 0)
    column = lax.broadcasted_iota(jnp.int32, (owners, count), 1)
    place = column - owner * whole
    inside = (place >= 0) & (place < whole) & (column < main)
    spread = jnp.where(inside | (column - main == owner), 1.0, 0.0)
    place = jnp.sum(jnp.where(inside, place, 0).astype(f32), axis=0, keepdims=True)
    last = lax.broadcasted_iota(jnp.int32, (1, count), 1) >= main
    place = jnp.where(last, float(whole), place)
    spread = spread.astype(bf16)
    row = lax.broadcasted_iota(jnp.int32, (row_count, row_count), 0)
    earlier = lax.broadcasted_iota(jnp.int32, (row_count, row_count), 1) < row
    below = jnp.where(earlier, 1.0, 0.0).astype(bf16)
    before = jnp.dot(below, hot.astype(bf16), preferred_element_type=f32)
    hot_c = jnp.dot(hot.astype(bf16), spread, preferred_element_type=f32)
    before_c = jnp.dot(before.astype(bf16), spread, preferred_element_type=f32)
    share_c = jnp.dot(share.astype(bf16), spread, preferred_element_type=f32)
    chosen = jnp.where(before_c == place, hot_c, 0.0)
    plain[...] = chosen.astype(bf16)
    weighted[...] = (chosen * share_c).astype(bf16)


def pallas(kernel, out_shape, scratch, name, *inputs, awaits=()):
    vmem = pl.BlockSpec(memory_space=pltpu.VMEM)

    def body(*refs):
        awaited, refs = refs[len(inputs) : len(inputs) + len(awaits)], (
            refs[: len(inputs)] + refs[len(inputs) + len(awaits) :]
        )
        if awaited:
            refs, (tile, sem) = refs[:-2], refs[-2:]
        for ref in awaited:
            part = (0,) * (len(ref.shape) - 2) + (pl.ds(0, 16), pl.ds(0, LANES))
            copy = pltpu.make_async_copy(ref.at[part], tile, sem)
            copy.start()
            copy.wait()
        kernel(*refs)

    if awaits:
        scratch = [*scratch, pltpu.VMEM((16, LANES), bf16), pltpu.SemaphoreType.DMA(())]

    return pl.pallas_call(
        body,
        out_shape=out_shape,
        in_specs=[vmem] * len(inputs) + [pl.BlockSpec(memory_space=pl.ANY)] * len(awaits),
        out_specs=jax.tree.map(lambda _: vmem, out_shape),
        scratch_shapes=scratch,
        compiler_params=pltpu.CompilerParams(vmem_limit_bytes=VMEM_BYTES),
        name=name,
    )(*inputs, *awaits)


def in_turn(value, awaited):
    def kernel(_, ref, out, tile, sem):
        part = (0,) * (len(ref.shape) - 2) + (pl.ds(0, 16), pl.ds(0, LANES))
        copy = pltpu.make_async_copy(ref.at[part], tile, sem)
        copy.start()
        copy.wait()

    anywhere = pl.BlockSpec(memory_space=pl.ANY)
    return pl.pallas_call(
        kernel,
        out_shape=jax.ShapeDtypeStruct(value.shape, value.dtype),
        in_specs=[anywhere] * 2,
        out_specs=anywhere,
        scratch_shapes=[pltpu.VMEM((16, LANES), bf16), pltpu.SemaphoreType.DMA(())],
        input_output_aliases={0: 0},
        name="in_turn",
    )(value, awaited)


def pack(table, rows, out, by_lane, tails):
    width = rows.shape[1]

    def step(i, s, n):
        value = lax.dot_general(
            table[...], rows[:, pl.ds(s, n)], (((0,), (0,)), ((), ())), preferred_element_type=f32
        )
        store_columns(out, by_lane, i, s, value)

    over_columns(width, step, unrolled=True)
    store_tails(out, by_lane, tails, width)


def normed(state_f):
    mean = jnp.mean(state_f * state_f, axis=-1, keepdims=True)
    inverse_rms = lax.rsqrt(mean + EPSILON)
    return state_f * inverse_rms, inverse_rms


def four(parts):
    own, far, left, right = (p[...].astype(f32) for p in parts)
    return (own + far) + (left + right)


def plain_kernel(rows, table, out, *tails):
    pack(table, rows, out, *tails)


def norm_kernel(x, gain, table, out, rows, *tails):
    rows[...] = (normed(x[...].astype(f32))[0] * gain[...]).astype(bf16)
    pack(table, rows, out, *tails)


def sum_norm_kernel(x, p0, p1, p2, p3, gain, table, following, out, rows, *tails):
    following[...] = (x[...].astype(f32) + four((p0, p1, p2, p3))).astype(bf16)
    rows[...] = (normed(following[...].astype(f32))[0] * gain[...]).astype(bf16)
    pack(table, rows, out, *tails)


def finish(x, upstream, parts, gain, grad):
    d_norm = four(parts)
    scaled, inverse_rms = normed(x[...].astype(f32))
    d_scaled = d_norm * gain[...]
    mean = jnp.mean(d_scaled * scaled, axis=-1, keepdims=True)
    d_input = inverse_rms * (d_scaled - scaled * mean)
    grad[...] = (upstream[...].astype(f32) + d_input).astype(bf16)
    return jnp.sum(d_norm * scaled, axis=0, keepdims=True)


def finish_kernel(x, upstream, p0, p1, p2, p3, gain, grad):
    finish(x, upstream, (p0, p1, p2, p3), gain, grad)


def finish_pack_kernel(x, upstream, p0, p1, p2, p3, gain, table, grad, out, gain_cols, *tails):
    gain_grad = finish(x, upstream, (p0, p1, p2, p3), gain, grad)
    for c in range(gain_cols.shape[0]):
        gain_cols[c : c + 1, :] = gain_grad[:, c * LANES : (c + 1) * LANES]
    pack(table, grad, out, *tails)
    store_gain(out, gain_cols, grad.shape[1])


def home_kernel(table, held, out, *refs):
    *summed, by_lane, tails = refs
    owners, whole, _ = held.shape
    width = out.shape[1]
    main = owners * whole
    tails[...] = held[:, :, width : width + LANES].astype(f32)
    for c in range(width // LANES):
        by_lane[c] = tails[:, c, :]

    def step(i, s, n):
        rows = held[:, :, pl.ds(s, n)].reshape(main, n)
        last = [by_lane[i * (n // LANES) + c] for c in range(n // LANES)]
        last = jnp.concatenate(last, axis=1).astype(bf16)
        value = jnp.dot(table[:, :main], rows, preferred_element_type=f32)
        value = value + jnp.dot(table[:, main:], last, preferred_element_type=f32)
        out[:, pl.ds(s, n)] = value.astype(bf16)

    over_columns(width, step, unrolled=True)
    for ref in summed:
        ref[...] = sum_gain(held, width)


def swapped(x):
    return lax.ppermute(x, "section", SWAP)


def after(value, first_done):
    return lax.optimization_barrier((value, first_done))[0]


def shards(inputs, cotangent, gain, w_up, w_down, expert_ids, expert_counts, combine_fixed):
    section = lax.axis_index("section")
    owners = lax.axis_size("dp")
    ring = lax.axis_size("expert")
    row_count, width = inputs.shape[1:]
    top = expert_ids.shape[3]
    capacity = min(row_count, row_count * top // owners + 1)
    whole = capacity - 1
    count = owners * capacity
    first = section == 0
    up_own, down_own = w_up[0, 0], w_down[0, 0]

    def like(*shape, dtype=bf16):
        return jax.ShapeDtypeStruct(shape, dtype)

    block = like(owners, whole, width + LANES)
    gain_block = like(owners, whole, width + 2 * LANES)
    cols_shape = like(width // LANES, LANES, dtype=f32)
    rows_shape = like(row_count, width)
    table_shape = like(row_count, count)
    tails = [
        pltpu.VMEM((width // LANES, owners, LANES), f32),
        pltpu.VMEM((owners, whole, LANES), f32),
    ]
    rows = pltpu.VMEM((row_count, width), bf16)

    def pick(mine, other, layer):
        return jnp.where(section == layer, mine, other)

    ints = jnp.concatenate([expert_ids[0], expert_counts[0][..., None], combine_fixed[0]], axis=-1)
    mine = lax.dynamic_index_in_dim(ints, section, 0, keepdims=False)
    theirs = swapped(lax.dynamic_index_in_dim(ints, 1 - section, 0, keepdims=False))
    gain_own = gain.astype(f32)
    gain_other = swapped(gain_own)
    x0 = lax.dynamic_index_in_dim(inputs, section, 0, keepdims=False)
    upstream = lax.dynamic_index_in_dim(cotangent, section, 0, keepdims=False)
    up_other, down_other = swapped(up_own), swapped(down_own)

    def tables(packed, *awaits):
        kernel = functools.partial(tables_kernel, top, whole)
        return pallas(kernel, [table_shape, table_shape], [], "tables", packed, awaits=awaits)

    def exchange(held):
        return lax.all_to_all(held, "dp", split_axis=0, concat_axis=0, tiled=True)

    def over_groups(part):
        pairs = [[(i, (i + by) % ring) for i in range(ring)] for by in (2, 1, 3)]
        return (part, *[lax.ppermute(part, "expert", p) for p in pairs])

    def home(table, held):
        return over_groups(pallas(home_kernel, [rows_shape], tails, "home", table, held)[0])

    weights = (up_own, down_own, up_other, down_other)

    def enter(current, gain_row, table, *awaits):
        args = (current, gain_row, table)
        return exchange(pallas(norm_kernel, block, [rows, *tails], "enter", *args, awaits=awaits))

    own_tables = tables(mine)
    rows0 = lax.cond(
        first,
        enter,
        lambda *a: jnp.zeros(block.shape, bf16),
        x0,
        gain_own,
        own_tables[0],
    )
    other_tables = tables(theirs, rows0)
    rows0 = lax.cond(
        first,
        lambda kept, *a: kept,
        lambda kept, *a: enter(*a),
        rows0,
        x0,
        gain_other,
        other_tables[0],
        up_other,
        down_other,
    )
    gain0, gain1 = (pick(gain_own, gain_other, layer) for layer in range(2))
    plain0, plain1 = (pick(own_tables[0], other_tables[0], layer) for layer in range(2))
    weighted0, weighted1 = (pick(own_tables[1], other_tables[1], layer) for layer in range(2))
    d_held1 = pallas(plain_kernel, block, tails, "spread", upstream, weighted1, awaits=(rows0,))
    d_rows1 = exchange(d_held1)

    part0, pre0 = expert("forward", 0, weights, rows0)
    back0 = exchange(in_turn(part0, d_rows1))
    sums0 = home(weighted0, back0)
    x1, held1 = pallas(
        sum_norm_kernel, [rows_shape, block], [rows, *tails], "next", x0, *sums0, gain1, plain1
    )
    rows1 = exchange(after(held1, d_rows1))
    part1, d_part1 = expert("both", 1, weights, rows1, d_rows1)
    d_back1 = exchange(d_part1)
    d_sums1 = home(plain1, d_back1)
    grad1, d_held0 = pallas(
        finish_pack_kernel,
        [rows_shape, gain_block],
        [pltpu.VMEM(cols_shape.shape, f32), *tails],
        "finish_next",
        x1,
        upstream,
        *d_sums1,
        gain1,
        weighted0,
    )
    d_rows0 = exchange(d_held0)
    back1 = exchange(in_turn(part1, d_rows0))
    d_part0, gain_sum1 = expert("backward", 0, weights, d_rows0, pre0, rows0, grad1)
    d_back0 = exchange(in_turn(d_part0, back1))
    x2 = (x1.astype(f32) + four(home(weighted1, back1))).astype(bf16)
    kept_x, taken_x = pick(x1, x2, 0), swapped(pick(x2, x1, 0))
    d_home0, gain_sum0 = pallas(
        home_kernel,
        [rows_shape, cols_shape],
        tails,
        "home_gain",
        plain0,
        d_back0,
        awaits=(taken_x,),
    )
    d_sums0 = over_groups(d_home0)
    gain_sum0 = four(over_groups(gain_sum0)) / gain0.reshape(cols_shape.shape)
    grad0 = pallas(finish_kernel, rows_shape, [], "finish", x0, grad1, *d_sums0, gain0)

    kept_g, taken_g = pick(grad0, grad1, 0), swapped(pick(grad1, grad0, 0))

    def gain_slice(summed):
        summed = summed.reshape(owners, width // owners)
        return lax.dynamic_index_in_dim(summed, lax.axis_index("dp"), 0, keepdims=False)

    slice0, slice1 = gain_slice(gain_sum0), gain_slice(gain_sum1)
    gain_sum = pick(slice0, slice1, 0) + swapped(pick(slice1, slice0, 0))

    def both(kept, taken):
        low, high = jnp.where(first, kept, taken), jnp.where(first, taken, kept)
        return jnp.stack([low, high])[None]

    return both(kept_x, taken_x), both(kept_g, taken_g), gain_sum[None]


def solution(mesh):
    return jax.shard_map(
        shards,
        mesh=mesh,
        in_specs=(
            P(None, "dp", None),
            P(None, "dp", None),
            P("section", None),
            P("section", "dp", "expert", None),
            P("section", "dp", "expert", None),
            P("section", None, "dp", None),
            P("section", None, "dp"),
            P("section", None, "dp", None),
        ),
        out_specs=(
            P("section", None, "dp", None),
            P("section", None, "dp", None),
            P("section", "dp"),
        ),
        check_vma=False,
    )
```
